256 devices in a mesh: wide: 64 (over y, x, z_hi), narrow: 4 (over z_lo, core).
Axes of the slice: x: 4, y: 4, z: 8 (z_hi: 4, z_lo: 2; z = z_hi * 2 + z_lo), core: 2. Of those that a mesh axis runs over, the one named last changes fastest.
Arguments:
- gradient: bfloat16 [3072, 12800], P('wide', 'narrow'), may hold values from -1 to 1
Outputs:
- update: bfloat16 [3072, 12800], P('wide', 'narrow')
The draws below stay inside these ranges and needn't reach their ends.
All inputs are finite; a program needn't handle non-finite values.
Results may differ from the reference program's by a relative error of at most 0.0059.
Values may be sent and summed in bfloat16 or wider, within the bound.
No kernel may reach another device: no remote copies, remote signals or barrier semaphores. Data moves between devices by JAX's collectives and lax.ppermute only.
A program may use at most 128 MiB of HBM per device.

```python
import math
import jax
import jax.numpy as jnp

ROWS = 3072
COLS = 12800


def draw_gradient(key, part):
    key = jax.random.fold_in(key, 7)
    noise_key, scale_key = jax.random.split(key)
    noise_part = jax.random.truncated_normal(noise_key, -4.0, 4.0, (ROWS, COLS), jnp.float32)
    row_scale = jax.random.uniform(scale_key, (ROWS, 1), jnp.float32, 0.85, 1.1)
    values = 0.7 / math.sqrt(float(COLS)) * row_scale * noise_part
    return values.astype(jnp.bfloat16)


def setup_inputs(seed: int = 0) -> dict:
    key_list = jax.random.split(jax.random.key(seed), 2)
    return {
        "gradient": draw_gradient(jax.random.fold_in(key_list[1], 71), 0),
    }


coef_a = 3.4445
coef_b = -4.775
coef_c = 2.0315

def reference(gradient):
    gram = jnp.dot(gradient, gradient.T, preferred_element_type=jnp.float32).astype(jnp.bfloat16)
    square = jnp.dot(gram, gram, preferred_element_type=jnp.float32)
    mixer = (coef_b * gram.astype(jnp.float32) + coef_c * square).astype(jnp.bfloat16)
    product = jnp.dot(mixer, gradient, preferred_element_type=jnp.float32)
    combined = coef_a * gradient.astype(jnp.float32) + product
    return (combined * math.sqrt(float(COLS))).astype(jnp.bfloat16)
```

```python
import functools
import math

import jax
import jax.numpy as jnp
import numpy as np
from jax import lax
from jax.experimental import pallas as pl
from jax.experimental.pallas import tpu as pltpu
from jax.sharding import Mesh, PartitionSpec as P

coef_a = 3.4445
coef_b = -4.775
coef_c = 2.0315

ALL = ("y", "x", "z", "zl", "core")
SIZES = (4, 4, 4, 2, 2)

STEP_MASKS = (4, 1, 12, 3)
Z_MASKS = ((1, 3), (3, 1))


def partners(function):
    pairs = []
    for i in range(math.prod(SIZES)):
        there = function(*(int(k) for k in np.unravel_index(i, SIZES)))
        pairs.append((i, int(np.ravel_multi_index(there, SIZES))))
    return pairs


def exchange(value, function):
    return lax.ppermute(value, ALL, partners(function))


def plane_mask(core, part, step):
    return STEP_MASKS[(step + 2 * core + part) % 4]


def swap_plane(value, part, step):
    def there(y, x, z, zl, core):
        mask = plane_mask(core, part, step)
        return y ^ (mask >> 2), x ^ (mask & 3), z, zl, core

    return exchange(value, there)


def swap_z(value, masks):
    return exchange(value, lambda y, x, z, zl, core: (y, x, z ^ masks[core], zl, core))


def swap_core(value):
    return exchange(value, lambda y, x, z, zl, core: (y, x, z, zl, core ^ 1))


def swap_zl(value):
    return exchange(value, lambda y, x, z, zl, core: (y, x, z, zl ^ 1, core))


def offsets(masks):
    found = [0]
    for mask in masks:
        found = found + [k ^ mask for k in found]
    return found


def order_kernel(rows, cuts, rows_idx, cols_idx, *refs):
    here, there = refs[-2:]
    for part in range(len(cuts) - 1):
        for half in range(2):
            ref = refs[2 * part + half]
            for k in range(8):
                at = pl.multiple_of(cols_idx[part, 8 * half + k] * rows, rows)
                there[pl.ds(at, rows), cuts[part] : cuts[part + 1]] = ref[
                    k * rows : (k + 1) * rows, :
                ]
    for half in range(2):
        ref = refs[2 * (len(cuts) - 1) + half]
        for k in range(2):
            at = pl.multiple_of(rows_idx[2 * half + k] * rows, rows)
            here[pl.ds(at, rows), :] = ref[k * rows : (k + 1) * rows, :]


def put_in_order(rows, cuts, rows_idx, cols_idx, pieces):
    columns = cuts[-1]
    smem = pl.BlockSpec(memory_space=pltpu.SMEM)
    vmem = pl.BlockSpec(memory_space=pltpu.VMEM)
    return pl.pallas_call(
        functools.partial(order_kernel, rows, cuts),
        out_shape=(
            jax.ShapeDtypeStruct((4 * rows, columns), jnp.bfloat16),
            jax.ShapeDtypeStruct((16 * rows, columns), jnp.bfloat16),
        ),
        in_specs=[smem, smem] + [vmem] * len(pieces),
        out_specs=(vmem, vmem),
        compiler_params=pltpu.CompilerParams(vmem_limit_bytes=32 * 1024 * 1024),
    )(rows_idx, cols_idx, *pieces)


def per_device(gradient):
    rows, cols = gradient.shape
    y, x, z = (lax.axis_index(k) for k in ("y", "x", "z"))
    zl, core = lax.axis_index("zl"), lax.axis_index("core")
    plane, member = y * 4 + x, zl * 2 + core

    middle = cols // 2 // 128 * 128
    cuts = (0, middle, cols)
    parts = [gradient[:, cuts[k] : cuts[k + 1]] for k in range(2)]
    gathered_z = jnp.concatenate([gradient, swap_z(gradient, (1, 3))], 0)
    for step in range(3):
        parts = [
            jnp.concatenate([value, swap_plane(value, part, step)], 0)
            for part, value in enumerate(parts)
        ]
    pieces = []
    for part, value in enumerate(parts):
        pieces += [value, swap_plane(value, part, 3)]
    pieces += [gathered_z, swap_z(gathered_z, (3, 1))]

    def table(make):
        return jnp.where(core == 0, jnp.array(make(0), jnp.int32), jnp.array(make(1), jnp.int32))

    cols_idx = plane ^ table(
        lambda c: [offsets([plane_mask(c, part, s) for s in range(4)]) for part in range(2)]
    )
    rows_idx = z ^ table(lambda c: offsets([Z_MASKS[c][0], Z_MASKS[c][1]]))
    own_rows, own_cols = put_in_order(rows, cuts, rows_idx, cols_idx, pieces)

    partial_gram = lax.dot_general(
        own_rows, own_cols, (((1,), (1,)), ((), ())), preferred_element_type=jnp.float32
    )
    partial_gram = partial_gram + swap_core(partial_gram)
    gram = partial_gram + swap_zl(partial_gram.astype(jnp.bfloat16)).astype(jnp.float32)
    gram = gram.astype(jnp.bfloat16)

    right = lax.dynamic_slice_in_dim(gram, (member ^ y ^ x) * rows, rows, 0)
    right = lax.all_to_all(
        jnp.broadcast_to(right[None], (16,) + right.shape), ("y", "x"), 0, 0
    ).reshape(16 * rows, 16 * rows)
    quarter = jnp.arange(4 * rows, dtype=jnp.int32)
    j, inside = quarter // rows, quarter % rows
    source = (j * 4 + (j ^ member ^ z)) * rows + inside
    everything = jnp.arange(16 * rows, dtype=jnp.int32)
    pick = (everything[:, None] == source[None, :]).astype(jnp.bfloat16)
    left = jnp.dot(gram, pick, preferred_element_type=jnp.float32).astype(jnp.bfloat16)
    lefts = [left] + [swap_z(left, (m, m)) for m in (1, 3, 2)]
    targets = [(j * 4 + (j ^ member ^ z ^ m)) * rows + inside for m in (0, 1, 3, 2)]
    place = (jnp.concatenate(targets)[:, None] == everything[None, :]).astype(jnp.bfloat16)
    left = jnp.dot(
        jnp.concatenate(lefts, 1), place, preferred_element_type=jnp.float32
    ).astype(jnp.bfloat16)
    square = jnp.dot(left, right, preferred_element_type=jnp.float32)
    square = square + swap_core(square)
    square = square + swap_zl(square.astype(jnp.bfloat16)).astype(jnp.float32)
    mixer = (coef_b * gram.astype(jnp.float32) + coef_c * square).astype(jnp.bfloat16)

    product = jnp.dot(mixer, own_cols, preferred_element_type=jnp.float32)

    def block(k):
        return lax.dynamic_slice_in_dim(product, k * rows, rows, 0)

    total = block(z)
    for m in (1, 3, 2):
        total = total + swap_z(block(z ^ m).astype(jnp.bfloat16), (m, m)).astype(jnp.float32)
    combined = coef_a * gradient.astype(jnp.float32) + total
    factor = math.sqrt(float(cols * 4))
    return (combined * factor).astype(jnp.bfloat16)


def solution(mesh):
    split = Mesh(mesh.devices.reshape(SIZES), ALL)
    spec = P(("y", "x", "z"), ("zl", "core"))
    return jax.shard_map(
        per_device, mesh=split, in_specs=(spec,), out_specs=spec, check_vma=False
    )
```

```python
import functools
import math

import jax
import jax.numpy as jnp
import numpy as np
from jax import lax
from jax.experimental import pallas as pl
from jax.experimental.pallas import tpu as pltpu
from jax.sharding import Mesh, PartitionSpec as P

coef_a = 3.4445
coef_b = -4.775
coef_c = 2.0315

ALL = ("y", "x", "z", "zl", "core")
SIZES = (4, 4, 4, 2, 2)

STEP_MASKS = (4, 1, 12, 3)
Z_MASKS = ((1, 3), (3, 1))


def partners(function):
    pairs = []
    for i in range(math.prod(SIZES)):
        there = function(*(int(k) for k in np.unravel_index(i, SIZES)))
        pairs.append((i, int(np.ravel_multi_index(there, SIZES))))
    return pairs


def exchange(value, function):
    return lax.ppermute(value, ALL, partners(function))


def plane_mask(core, part, step):
    return STEP_MASKS[(step + 2 * core + part) % 4]


def swap_plane(value, part, step):
    def there(y, x, z, zl, core):
        mask = plane_mask(core, part, step)
        return y ^ (mask >> 2), x ^ (mask & 3), z, zl, core

    return exchange(value, there)


def swap_z(value, masks):
    return exchange(value, lambda y, x, z, zl, core: (y, x, z ^ masks[core], zl, core))


def swap_core(value):
    return exchange(value, lambda y, x, z, zl, core: (y, x, z, zl, core ^ 1))


def swap_zl(value):
    return exchange(value, lambda y, x, z, zl, core: (y, x, z, zl ^ 1, core))


def offsets(masks):
    found = [0]
    for mask in masks:
        found = found + [k ^ mask for k in found]
    return found


def multiply(a, b, dims):
    return lax.dot_general(a, b, (dims, ((), ())), preferred_element_type=jnp.float32)


def gram_kernel(rows, at_rows, at_cols, at_core, c00, c01, c10, c11, near, far, *refs):
    keep, give, own, flip = refs
    for half, ref in enumerate((near, far)):
        for k in range(2):
            at = pl.multiple_of(at_rows[2 * half + k] * rows, rows)
            own[pl.ds(at, rows), :] = ref[k * rows : (k + 1) * rows, :]
    flip[:, 4 * rows :] = jnp.zeros((16 * rows, flip.shape[1] - 4 * rows), jnp.float32)
    start = 0
    for part, halves in enumerate(((c00, c01), (c10, c11))):
        width = halves[0].shape[1]
        for half in range(2):
            block = multiply(halves[half][...], own[:, start : start + width], ((1,), (1,)))
            for k in range(8):
                at = pl.multiple_of(at_cols[part, 8 * half + k] * rows, rows)
                value = block[k * rows : (k + 1) * rows, :]
                if part > 0:
                    value = value + flip[pl.ds(at, rows), 0 : 4 * rows]
                flip[pl.ds(at, rows), 0 : 4 * rows] = value
        start += width
    gram = flip[...].T
    first = at_core[0] == 0
    keep[...] = jnp.where(first, gram[0 : 2 * rows], gram[2 * rows : 4 * rows])
    give[...] = jnp.where(first, gram[2 * rows : 4 * rows], gram[0 : 2 * rows])


def gram_halves(rows, at_rows, at_cols, at_core, pieces):
    smem = pl.BlockSpec(memory_space=pltpu.SMEM)
    vmem = pl.BlockSpec(memory_space=pltpu.VMEM)
    half = jax.ShapeDtypeStruct((2 * rows, 16 * rows), jnp.float32)
    padded = (4 * rows + 127) // 128 * 128
    return pl.pallas_call(
        functools.partial(gram_kernel, rows),
        out_shape=(half, half),
        in_specs=[smem] * 3 + [vmem] * 6,
        out_specs=(vmem, vmem),
        scratch_shapes=[
            pltpu.VMEM((4 * rows, pieces[-1].shape[1]), jnp.bfloat16),
            pltpu.VMEM((16 * rows, padded), jnp.float32),
        ],
        compiler_params=pltpu.CompilerParams(vmem_limit_bytes=16 * 1024 * 1024),
    )(at_rows, at_cols, at_core, *pieces)


def mixer_kernel(rows, at_rows, at_cols, at_core, mine, other, *refs):
    outputs, (straight, flip) = refs[:2], refs[2:]
    for k in range(2):
        for half, ref in enumerate((mine, other)):
            place = at_rows[2 * (at_core[0] ^ half) + k]
            at = pl.multiple_of(place * rows, rows)
            straight[pl.ds(at, rows), :] = ref[k * rows : (k + 1) * rows, :].astype(jnp.float32)
    straight[4 * rows :, :] = jnp.zeros((straight.shape[0] - 4 * rows, 16 * rows), jnp.float32)
    flip[...] = straight[...].T.astype(jnp.bfloat16)
    for part, ref in enumerate(outputs):
        for k in range(16):
            at = pl.multiple_of(at_cols[part, k] * rows, rows)
            ref[k * rows : (k + 1) * rows, :] = flip[pl.ds(at, rows), 0 : 4 * rows]


def mixer_parts(rows, at_rows, at_cols, at_core, mine, other):
    smem = pl.BlockSpec(memory_space=pltpu.SMEM)
    vmem = pl.BlockSpec(memory_space=pltpu.VMEM)
    shape = jax.ShapeDtypeStruct((16 * rows, 4 * rows), jnp.bfloat16)
    padded = (4 * rows + 127) // 128 * 128
    return pl.pallas_call(
        functools.partial(mixer_kernel, rows),
        out_shape=(shape, shape),
        in_specs=[smem] * 3 + [vmem] * 2,
        out_specs=(vmem, vmem),
        scratch_shapes=[
            pltpu.VMEM((padded, 16 * rows), jnp.float32),
            pltpu.VMEM((16 * rows, padded), jnp.bfloat16),
        ],
        compiler_params=pltpu.CompilerParams(vmem_limit_bytes=8 * 1024 * 1024),
    )(at_rows, at_cols, at_core, mine, other)


def pick(value, at, axis):
    return lax.dynamic_index_in_dim(value, at, axis, keepdims=False)


def per_device(gradient):
    rows, cols = gradient.shape
    y, x, z = (lax.axis_index(k) for k in ("y", "x", "z"))
    zl, core = lax.axis_index("zl"), lax.axis_index("core")
    plane, member = y * 4 + x, zl * 2 + core

    middle = cols // 2 // 128 * 128
    over_z = jnp.concatenate([gradient, swap_z(gradient, (1, 3))], 0)
    parts = [gradient[:, :middle], gradient[:, middle:]]
    for step in range(3):
        parts = [
            jnp.concatenate([value, swap_plane(value, part, step)], 0)
            for part, value in enumerate(parts)
        ]
    pieces = []
    for part, value in enumerate(parts):
        pieces += [value, swap_plane(value, part, 3)]
    pieces += [over_z, swap_z(over_z, (3, 1))]

    def table(make):
        return jnp.where(core == 0, jnp.array(make(0), jnp.int32), jnp.array(make(1), jnp.int32))

    at_cols = plane ^ table(
        lambda c: [offsets([plane_mask(c, part, s) for s in range(4)]) for part in range(2)]
    )
    at_rows = z ^ table(lambda c: offsets([Z_MASKS[c][0], Z_MASKS[c][1]]))
    at_core = core.astype(jnp.int32).reshape(1)
    width = 16 * rows
    gram_half, given = gram_halves(rows, at_rows, at_cols, at_core, pieces)
    gram_half = gram_half + swap_core(given)
    gram_half = (gram_half + swap_zl(gram_half)).astype(jnp.bfloat16)
    other = swap_core(gram_half)
    gram = jnp.where(
        core == 0, jnp.concatenate([gram_half, other]), jnp.concatenate([other, gram_half])
    )

    def partner(y, x, z, zl, core):
        return y, x, z ^ (2 * zl + core), zl, core

    left = exchange(gram, partner)
    right = lax.dynamic_slice_in_dim(gram, (z ^ member) * rows, rows, 0)
    right = lax.all_to_all(
        jnp.broadcast_to(right[None], (16, rows, width)), ("y", "x"), 0, 0
    ).reshape(width, width)
    square = jnp.dot(left, right, preferred_element_type=jnp.float32)
    square = square.reshape(2, 2 * rows, width)
    square = pick(square, core, 0) + swap_core(pick(square, 1 - core, 0))
    square = square + swap_zl(square.astype(jnp.bfloat16)).astype(jnp.float32)
    mixer = (coef_b * gram_half.astype(jnp.float32) + coef_c * square).astype(jnp.bfloat16)
    flips = mixer_parts(
        rows, z ^ jnp.arange(4, dtype=jnp.int32), at_cols, at_core, mixer, swap_core(mixer)
    )

    sums = []
    for part, flip in enumerate(flips):
        product = sum(
            multiply(flip[8 * rows * k : 8 * rows * (k + 1)], pieces[2 * part + k], ((0,), (0,)))
            for k in range(2)
        )
        product = product.reshape(4, rows, product.shape[1])
        near = jnp.where(core == 0, product[1], product[3])
        far = jnp.where(core == 0, product[3], product[1])
        moved = swap_z(jnp.stack([far, product[2]]).astype(jnp.bfloat16), (3, 1))
        moved = moved.astype(jnp.float32)
        last = swap_z((near + moved[1]).astype(jnp.bfloat16), (1, 3))
        sums.append(product[0] + moved[0] + last.astype(jnp.float32))
    combined = coef_a * gradient.astype(jnp.float32) + jnp.concatenate(sums, 1)
    factor = math.sqrt(float(cols * 4))
    return (combined * factor).astype(jnp.bfloat16)


def solution(mesh):
    split = Mesh(mesh.devices.reshape(SIZES), ALL)
    spec = P(("y", "x", "z"), ("zl", "core"))
    return jax.shard_map(
        per_device, mesh=split, in_specs=(spec,), out_specs=spec, check_vma=False
    )
```

```python
import functools
import math

import jax
import jax.numpy as jnp
import numpy as np
from jax import lax
from jax.experimental import pallas as pl
from jax.experimental.pallas import tpu as pltpu
from jax.sharding import Mesh, PartitionSpec as P

coef_a = 3.4445
coef_b = -4.775
coef_c = 2.0315

ALL = ("y", "x", "z", "zl", "core")
SIZES = (4, 4, 4, 2, 2)

STEP_MASKS = (4, 1, 12, 3)
Z_MASKS = ((1, 3), (3, 1))


def partners(function):
    pairs = []
    for i in range(math.prod(SIZES)):
        there = function(*(int(k) for k in np.unravel_index(i, SIZES)))
        pairs.append((i, int(np.ravel_multi_index(there, SIZES))))
    return pairs


def exchange(value, function):
    return lax.ppermute(value, ALL, partners(function))


def plane_mask(core, part, step):
    return STEP_MASKS[(step + 2 * core + part) % 4]


def swap_plane(value, part, step):
    def there(y, x, z, zl, core):
        mask = plane_mask(core, part, step)
        return y ^ (mask >> 2), x ^ (mask & 3), z, zl, core

    return exchange(value, there)


def swap_z(value, masks):
    return exchange(value, lambda y, x, z, zl, core: (y, x, z ^ masks[core], zl, core))


def swap_core(value):
    return exchange(value, lambda y, x, z, zl, core: (y, x, z, zl, core ^ 1))


def swap_zl(value):
    return exchange(value, lambda y, x, z, zl, core: (y, x, z, zl ^ 1, core))


def offsets(masks):
    found = [0]
    for mask in masks:
        found = found + [k ^ mask for k in found]
    return found


def multiply(a, b, dims):
    return lax.dot_general(a, b, (dims, ((), ())), preferred_element_type=jnp.float32)


def gram_kernel(rows, at_rows, at_cols, at_half, c00, c01, c10, c11, near, far, *refs):
    keep, give, own, flip = refs
    for half, ref in enumerate((near, far)):
        for k in range(2):
            at = pl.multiple_of(at_rows[2 * half + k] * rows, rows)
            own[pl.ds(at, rows), :] = ref[k * rows : (k + 1) * rows, :]
    flip[:, 4 * rows :] = jnp.zeros((16 * rows, flip.shape[1] - 4 * rows), jnp.float32)
    start = 0
    for part, halves in enumerate(((c00, c01), (c10, c11))):
        width = halves[0].shape[1]
        for half in range(2):
            block = multiply(halves[half][...], own[:, start : start + width], ((1,), (1,)))
            for k in range(8):
                at = pl.multiple_of(at_cols[part, 8 * half + k] * rows, rows)
                value = block[k * rows : (k + 1) * rows, :]
                if part > 0:
                    value = value + flip[pl.ds(at, rows), 0 : 4 * rows]
                flip[pl.ds(at, rows), 0 : 4 * rows] = value
        start += width
    gram = flip[...].T
    first = at_half[0] == 0
    keep[...] = jnp.where(first, gram[0 : 2 * rows], gram[2 * rows : 4 * rows])
    give[...] = jnp.where(first, gram[2 * rows : 4 * rows], gram[0 : 2 * rows])


def gram_halves(rows, at_rows, at_cols, at_half, pieces):
    smem = pl.BlockSpec(memory_space=pltpu.SMEM)
    vmem = pl.BlockSpec(memory_space=pltpu.VMEM)
    half = jax.ShapeDtypeStruct((2 * rows, 16 * rows), jnp.float32)
    padded = (4 * rows + 127) // 128 * 128
    return pl.pallas_call(
        functools.partial(gram_kernel, rows),
        out_shape=(half, half),
        in_specs=[smem] * 3 + [vmem] * 6,
        out_specs=(vmem, vmem),
        scratch_shapes=[
            pltpu.VMEM((4 * rows, pieces[-1].shape[1]), jnp.bfloat16),
            pltpu.VMEM((16 * rows, padded), jnp.float32),
        ],
        compiler_params=pltpu.CompilerParams(vmem_limit_bytes=16 * 1024 * 1024),
    )(at_rows, at_cols, at_half, *pieces)


def mixer_kernel(rows, at_rows, at_cols, at_half, mine, other, *refs):
    outputs, (straight, flip, moved) = refs[:2], refs[2:]
    for k in range(2):
        for half, ref in enumerate((mine, other)):
            place = at_rows[2 * (at_half[0] ^ half) + k]
            at = pl.multiple_of(place * rows, rows)
            straight[pl.ds(at, rows), :] = ref[k * rows : (k + 1) * rows, :].astype(jnp.float32)
    straight[4 * rows :, :] = jnp.zeros((straight.shape[0] - 4 * rows, 16 * rows), jnp.float32)
    flip[...] = straight[...].T
    for part, ref in enumerate(outputs):
        for k in range(16):
            at = pl.multiple_of(at_cols[part, k] * rows, rows)
            moved[k * rows : (k + 1) * rows, :] = flip[pl.ds(at, rows), :]
        ref[...] = moved[...].T[0 : 4 * rows].astype(jnp.bfloat16)


def mixer_parts(rows, at_rows, at_cols, at_half, mine, other):
    smem = pl.BlockSpec(memory_space=pltpu.SMEM)
    vmem = pl.BlockSpec(memory_space=pltpu.VMEM)
    shape = jax.ShapeDtypeStruct((4 * rows, 16 * rows), jnp.bfloat16)
    padded = (4 * rows + 127) // 128 * 128
    return pl.pallas_call(
        functools.partial(mixer_kernel, rows),
        out_shape=(shape, shape),
        in_specs=[smem] * 3 + [vmem] * 2,
        out_specs=(vmem, vmem),
        scratch_shapes=[
            pltpu.VMEM((padded, 16 * rows), jnp.float32),
            pltpu.VMEM((16 * rows, padded), jnp.float32),
            pltpu.VMEM((16 * rows, padded), jnp.float32),
        ],
        compiler_params=pltpu.CompilerParams(vmem_limit_bytes=8 * 1024 * 1024),
    )(at_rows, at_cols, at_half, mine, other)


def pick(value, at, axis):
    return lax.dynamic_index_in_dim(value, at, axis, keepdims=False)


def per_device(gradient):
    rows, cols = gradient.shape
    y, x, z = (lax.axis_index(k) for k in ("y", "x", "z"))
    zl, core = lax.axis_index("zl"), lax.axis_index("core")
    plane = y * 4 + x

    middle = cols // 2 // 128 * 128
    over_z = jnp.concatenate([gradient, swap_z(gradient, (1, 3))], 0)
    parts = [gradient[:, :middle], gradient[:, middle:]]
    for step in range(3):
        parts = [
            jnp.concatenate([value, swap_plane(value, part, step)], 0)
            for part, value in enumerate(parts)
        ]
    pieces = []
    for part, value in enumerate(parts):
        pieces += [value, swap_plane(value, part, 3)]
    pieces += [over_z, swap_z(over_z, (3, 1))]

    def table(make):
        return jnp.where(core == 0, jnp.array(make(0), jnp.int32), jnp.array(make(1), jnp.int32))

    at_cols = plane ^ table(
        lambda c: [offsets([plane_mask(c, part, s) for s in range(4)]) for part in range(2)]
    )
    at_rows = z ^ table(lambda c: offsets([Z_MASKS[c][0], Z_MASKS[c][1]]))
    half = core ^ (z >> 1)
    at_half = half.astype(jnp.int32).reshape(1)
    width = 16 * rows

    row = jnp.arange(2 * rows, dtype=jnp.int32)
    diagonal = jnp.where(2 * half + row // rows == z, plane * rows + row % rows, -1)
    diagonal = diagonal[:, None] == jnp.arange(width, dtype=jnp.int32)[None, :]

    def add_zl(value):
        rounded = lax.reduce_precision(value, 8, 7)
        rest = jnp.sum(jnp.where(diagonal, value - rounded, 0.0), 0, keepdims=True)
        rest = jnp.broadcast_to(rest, (16, width))
        sent = jnp.concatenate([rounded, rest]).astype(jnp.bfloat16)
        got = swap_zl(sent).astype(jnp.float32)
        return value + got[: 2 * rows] + jnp.where(diagonal, got[2 * rows : 2 * rows + 1], 0.0)

    gram_half, given = gram_halves(rows, at_rows, at_cols, at_half, pieces)
    gram_half = add_zl(gram_half + swap_core(given)).astype(jnp.bfloat16)

    right = pick(gram_half.reshape(2, rows, width), zl ^ (z & 1), 0)
    right = lax.all_to_all(
        jnp.broadcast_to(right[None], (16, rows, width)), ("y", "x"), 0, 0
    ).reshape(width, width)
    other = swap_core(gram_half)
    left = exchange(
        jnp.where(
            half == 0, jnp.concatenate([gram_half, other]), jnp.concatenate([other, gram_half])
        ),
        lambda y, x, z, zl, core: (y, x, z ^ (2 * core + zl), zl, core),
    )
    square = jnp.dot(left, right, preferred_element_type=jnp.float32)
    square = square.reshape(2, 2 * rows, width)
    square = add_zl(pick(square, half, 0) + swap_core(pick(square, 1 - half, 0)))
    mixer = (coef_b * gram_half.astype(jnp.float32) + coef_c * square).astype(jnp.bfloat16)
    mixers = mixer_parts(
        rows, z ^ jnp.arange(4, dtype=jnp.int32), at_cols, at_half, mixer, swap_core(mixer)
    )

    sums = []
    for part, block in enumerate(mixers):
        product = jnp.dot(
            block[:, : 8 * rows], pieces[2 * part], preferred_element_type=jnp.float32
        ) + jnp.dot(
            block[:, 8 * rows :], pieces[2 * part + 1], preferred_element_type=jnp.float32
        )
        product = product.reshape(4, rows, product.shape[1])
        near = jnp.where(core == 0, product[1], product[3])
        far = jnp.where(core == 0, product[3], product[1])
        moved = swap_z(jnp.stack([far, product[2]]).astype(jnp.bfloat16), (3, 1))
        moved = moved.astype(jnp.float32)
        last = swap_z((near + moved[1]).astype(jnp.bfloat16), (1, 3))
        sums.append(product[0] + moved[0] + last.astype(jnp.float32))
    combined = coef_a * gradient.astype(jnp.float32) + jnp.concatenate(sums, 1)
    factor = math.sqrt(float(cols * 4))
    return (combined * factor).astype(jnp.bfloat16)


def solution(mesh):
    split = Mesh(mesh.devices.reshape(SIZES), ALL)
    spec = P(("y", "x", "z"), ("zl", "core"))
    return jax.shard_map(
        per_device, mesh=split, in_specs=(spec,), out_specs=spec, check_vma=False
    )
```

```python
import functools
import math

import jax
import jax.numpy as jnp
import numpy as np
from jax import lax
from jax.experimental import pallas as pl
from jax.experimental.pallas import tpu as pltpu
from jax.sharding import Mesh, PartitionSpec as P

coef_a = 3.4445
coef_b = -4.775
coef_c = 2.0315

ALL = ("y", "x", "z", "zl", "core")
SIZES = (4, 4, 4, 2, 2)

STEP_MASKS = (4, 1, 12, 3)
Z_MASKS = ((1, 3), (3, 1))


def partners(function):
    pairs = []
    for i in range(math.prod(SIZES)):
        there = function(*(int(k) for k in np.unravel_index(i, SIZES)))
        pairs.append((i, int(np.ravel_multi_index(there, SIZES))))
    return pairs


def exchange(value, function):
    return lax.ppermute(value, ALL, partners(function))


def plane_mask(core, part, step):
    return STEP_MASKS[(step + 2 * core + part) % 4]


def swap_plane(value, part, step):
    def there(y, x, z, zl, core):
        mask = plane_mask(core, part, step)
        return y ^ (mask >> 2), x ^ (mask & 3), z, zl, core

    return exchange(value, there)


def swap_z(value, masks):
    return exchange(value, lambda y, x, z, zl, core: (y, x, z ^ masks[core], zl, core))


def swap_core(value):
    return exchange(value, lambda y, x, z, zl, core: (y, x, z, zl, core ^ 1))


def swap_zl(value):
    return exchange(value, lambda y, x, z, zl, core: (y, x, z, zl ^ 1, core))


def offsets(masks):
    found = [0]
    for mask in masks:
        found = found + [k ^ mask for k in found]
    return found


def multiply(a, b, dims):
    return lax.dot_general(a, b, (dims, ((), ())), preferred_element_type=jnp.float32)


def position():
    y, x, z, core = (lax.axis_index(k) for k in ("y", "x", "z", "core"))
    return y * 4 + x, z, core


def gathered_places(part):
    plane, _, core = position()
    orders = [offsets([plane_mask(c, part, step) for step in range(4)]) for c in range(2)]
    return [plane ^ jnp.where(core == 0, *pair) for pair in zip(*orders)]


def kept_half():
    _, z, core = position()
    return core ^ (z >> 1)


def gram_kernel(rows, c00, c01, c10, c11, near, far, *refs):
    keep, give, own, flip = refs
    _, z, core = position()
    orders = [offsets(masks) for masks in Z_MASKS]
    for k, pair in enumerate(zip(*orders)):
        at = pl.multiple_of((z ^ jnp.where(core == 0, *pair)) * rows, rows)
        ref = (near, far)[k // 2]
        own[pl.ds(at, rows), :] = ref[(k % 2) * rows : (k % 2 + 1) * rows, :]
    flip[:, 4 * rows :] = jnp.zeros((16 * rows, flip.shape[1] - 4 * rows), jnp.float32)
    start = 0
    for part, halves in enumerate(((c00, c01), (c10, c11))):
        width = halves[0].shape[1]
        places = gathered_places(part)
        for half in range(2):
            block = multiply(halves[half][...], own[:, start : start + width], ((1,), (1,)))
            for k in range(8):
                at = pl.multiple_of(places[8 * half + k] * rows, rows)
                value = block[k * rows : (k + 1) * rows, :]
                if part > 0:
                    value = value + flip[pl.ds(at, rows), 0 : 4 * rows]
                flip[pl.ds(at, rows), 0 : 4 * rows] = value
        start += width
    gram = flip[...].T
    first = kept_half() == 0
    keep[...] = jnp.where(first, gram[0 : 2 * rows], gram[2 * rows : 4 * rows])
    give[...] = jnp.where(first, gram[2 * rows : 4 * rows], gram[0 : 2 * rows])


def gram_halves(rows, pieces):
    vmem = pl.BlockSpec(memory_space=pltpu.VMEM)
    half = jax.ShapeDtypeStruct((2 * rows, 16 * rows), jnp.float32)
    padded = (4 * rows + 127) // 128 * 128
    return pl.pallas_call(
        functools.partial(gram_kernel, rows),
        out_shape=(half, half),
        in_specs=[vmem] * 6,
        out_specs=(vmem, vmem),
        scratch_shapes=[
            pltpu.VMEM((4 * rows, pieces[-1].shape[1]), jnp.bfloat16),
            pltpu.VMEM((16 * rows, padded), jnp.float32),
        ],
        compiler_params=pltpu.CompilerParams(vmem_limit_bytes=16 * 1024 * 1024),
    )(*pieces)


def mixer_kernel(rows, mine, other, *refs):
    outputs, (straight, flip, moved) = refs[:2], refs[2:]
    _, z, _ = position()
    for k in range(2):
        for half, ref in enumerate((mine, other)):
            at = pl.multiple_of(((2 * (kept_half() ^ half) + k) ^ z) * rows, rows)
            straight[pl.ds(at, rows), :] = ref[k * rows : (k + 1) * rows, :].astype(jnp.float32)
    straight[4 * rows :, :] = jnp.zeros((straight.shape[0] - 4 * rows, 16 * rows), jnp.float32)
    flip[...] = straight[...].T
    for part, ref in enumerate(outputs):
        for k, place in enumerate(gathered_places(part)):
            at = pl.multiple_of(place * rows, rows)
            moved[k * rows : (k + 1) * rows, :] = flip[pl.ds(at, rows), :]
        ref[...] = moved[...].T[0 : 4 * rows].astype(jnp.bfloat16)


def mixer_parts(rows, mine, other):
    vmem = pl.BlockSpec(memory_space=pltpu.VMEM)
    shape = jax.ShapeDtypeStruct((4 * rows, 16 * rows), jnp.bfloat16)
    padded = (4 * rows + 127) // 128 * 128
    return pl.pallas_call(
        functools.partial(mixer_kernel, rows),
        out_shape=(shape, shape),
        in_specs=[vmem] * 2,
        out_specs=(vmem, vmem),
        scratch_shapes=[
            pltpu.VMEM((padded, 16 * rows), jnp.float32),
            pltpu.VMEM((16 * rows, padded), jnp.float32),
            pltpu.VMEM((16 * rows, padded), jnp.float32),
        ],
        compiler_params=pltpu.CompilerParams(vmem_limit_bytes=8 * 1024 * 1024),
    )(mine, other)


def per_device(gradient):
    rows, cols = gradient.shape
    y, x, z = (lax.axis_index(k) for k in ("y", "x", "z"))
    zl, core = lax.axis_index("zl"), lax.axis_index("core")
    plane = y * 4 + x

    half = core ^ (z >> 1)
    choices = (half == 0, zl == (z & 1), core == 0, (z - 2 * half) * rows, plane * rows)
    gradient, choices = lax.optimization_barrier((gradient, choices))
    first_half, first_block, first_core, first_row, first_column = choices

    middle = cols // 2 // 128 * 128
    over_z = jnp.concatenate([gradient, swap_z(gradient, (1, 3))], 0)
    parts = [gradient[:, :middle], gradient[:, middle:]]
    for step in range(3):
        parts = [
            jnp.concatenate([value, swap_plane(value, part, step)], 0)
            for part, value in enumerate(parts)
        ]
    pieces = []
    for part, value in enumerate(parts):
        pieces += [value, swap_plane(value, part, 3)]
    pieces += [over_z, swap_z(over_z, (3, 1))]
    pieces = lax.optimization_barrier(pieces)

    width = 16 * rows

    row = lax.broadcasted_iota(jnp.int32, (2 * rows, width), 0) - first_row
    column = lax.broadcasted_iota(jnp.int32, (2 * rows, width), 1) - first_column
    diagonal = (row == column) & (row >= 0) & (row < rows)

    def add_zl(value):
        rounded = lax.reduce_precision(value, 8, 7)
        rest = jnp.sum(jnp.where(diagonal, value - rounded, 0.0), 0, keepdims=True)
        rest = jnp.broadcast_to(rest, (16, width))
        sent = jnp.concatenate([rounded, rest]).astype(jnp.bfloat16)
        got = swap_zl(sent).astype(jnp.float32)
        return value + got[: 2 * rows] + jnp.where(diagonal, got[2 * rows : 2 * rows + 1], 0.0)

    gram_half, given = gram_halves(rows, pieces)
    gram_half = add_zl(gram_half + swap_core(given)).astype(jnp.bfloat16)

    right = jnp.where(first_block, gram_half[:rows], gram_half[rows:])
    right = lax.all_to_all(
        jnp.broadcast_to(right[None], (16, rows, width)), ("y", "x"), 0, 0
    ).reshape(width, width)
    other = swap_core(gram_half)
    left = exchange(
        jnp.where(
            first_half, jnp.concatenate([gram_half, other]), jnp.concatenate([other, gram_half])
        ),
        lambda y, x, z, zl, core: (y, x, z ^ (2 * core + zl), zl, core),
    )
    square = jnp.dot(left, right, preferred_element_type=jnp.float32)
    halves = square[: 2 * rows], square[2 * rows :]
    square = jnp.where(first_half, halves[0], halves[1])
    square = add_zl(square + swap_core(jnp.where(first_half, halves[1], halves[0])))
    mixer = (coef_b * gram_half.astype(jnp.float32) + coef_c * square).astype(jnp.bfloat16)
    mixers = mixer_parts(rows, mixer, swap_core(mixer))

    sums = []
    for part, block in enumerate(mixers):
        product = jnp.dot(
            block[:, : 8 * rows], pieces[2 * part], preferred_element_type=jnp.float32
        ) + jnp.dot(
            block[:, 8 * rows :], pieces[2 * part + 1], preferred_element_type=jnp.float32
        )
        product = product.reshape(4, rows, product.shape[1])
        near = jnp.where(first_core, product[1], product[3])
        far = jnp.where(first_core, product[3], product[1])
        moved = swap_z(jnp.stack([far, product[2]]).astype(jnp.bfloat16), (3, 1))
        moved = moved.astype(jnp.float32)
        last = swap_z((near + moved[1]).astype(jnp.bfloat16), (1, 3))
        sums.append(product[0] + moved[0] + last.astype(jnp.float32))
    combined = coef_a * gradient.astype(jnp.float32) + jnp.concatenate(sums, 1)
    factor = math.sqrt(float(cols * 4))
    return (combined * factor).astype(jnp.bfloat16)


def solution(mesh):
    split = Mesh(mesh.devices.reshape(SIZES), ALL)
    spec = P(("y", "x", "z"), ("zl", "core"))
    return jax.shard_map(
        per_device, mesh=split, in_specs=(spec,), out_specs=spec, check_vma=False
    )
```

```python
import functools
import math

import jax
import jax.numpy as jnp
import numpy as np
from jax import lax
from jax.experimental import pallas as pl
from jax.experimental.pallas import tpu as pltpu
from jax.sharding import Mesh, PartitionSpec as P

coef_a = 3.4445
coef_b = -4.775
coef_c = 2.0315

ALL = ("y", "x", "z", "zl", "core")
SIZES = (4, 4, 4, 2, 2)

STEP_MASKS = (4, 1, 12, 3)
Z_MASKS = ((1, 3), (3, 1))


def partners(function):
    pairs = []
    for i in range(math.prod(SIZES)):
        there = function(*(int(k) for k in np.unravel_index(i, SIZES)))
        pairs.append((i, int(np.ravel_multi_index(there, SIZES))))
    return pairs


def exchange(value, function):
    return lax.ppermute(value, ALL, partners(function))


def plane_mask(core, part, step):
    return STEP_MASKS[(step + 2 * core + part) % 4]


def swap_plane(value, part, step):
    def there(y, x, z, zl, core):
        mask = plane_mask(core, part, step)
        return y ^ (mask >> 2), x ^ (mask & 3), z, zl, core

    return exchange(value, there)


def swap_z(value, masks):
    return exchange(value, lambda y, x, z, zl, core: (y, x, z ^ masks[core], zl, core))


def swap_core(value):
    return exchange(value, lambda y, x, z, zl, core: (y, x, z, zl, core ^ 1))


def swap_zl(value):
    return exchange(value, lambda y, x, z, zl, core: (y, x, z, zl ^ 1, core))


def offsets(masks):
    found = [0]
    for mask in masks:
        found = found + [k ^ mask for k in found]
    return found


def multiply(a, b, dims):
    return lax.dot_general(a, b, (dims, ((), ())), preferred_element_type=jnp.float32)


def position():
    y, x, z, core = (lax.axis_index(k) for k in ("y", "x", "z", "core"))
    return y * 4 + x, z, core


def gathered_places(part):
    plane, _, core = position()
    orders = [offsets([plane_mask(c, part, step) for step in range(4)]) for c in range(2)]
    return [plane ^ jnp.where(core == 0, *pair) for pair in zip(*orders)]


def kept_half():
    _, z, core = position()
    return core ^ (z >> 1)


def gram_kernel(rows, c00, c01, c10, c11, near, far, *refs):
    keep, give, own, flip = refs
    _, z, core = position()
    orders = [offsets(masks) for masks in Z_MASKS]
    for k, pair in enumerate(zip(*orders)):
        at = pl.multiple_of((z ^ jnp.where(core == 0, *pair)) * rows, rows)
        ref = (near, far)[k // 2]
        own[pl.ds(at, rows), :] = ref[(k % 2) * rows : (k % 2 + 1) * rows, :]
    flip[:, 4 * rows :] = jnp.zeros((16 * rows, flip.shape[1] - 4 * rows), jnp.float32)
    start = 0
    for part, halves in enumerate(((c00, c01), (c10, c11))):
        width = halves[0].shape[1]
        places = gathered_places(part)
        for half in range(2):
            block = multiply(halves[half][...], own[:, start : start + width], ((1,), (1,)))
            for k in range(8):
                at = pl.multiple_of(places[8 * half + k] * rows, rows)
                value = block[k * rows : (k + 1) * rows, :]
                if part > 0:
                    value = value + flip[pl.ds(at, rows), 0 : 4 * rows]
                flip[pl.ds(at, rows), 0 : 4 * rows] = value
        start += width
    gram = flip[...].T
    first = kept_half() == 0
    keep[...] = jnp.where(first, gram[0 : 2 * rows], gram[2 * rows : 4 * rows])
    give[...] = jnp.where(first, gram[2 * rows : 4 * rows], gram[0 : 2 * rows])


def gram_halves(rows, pieces):
    vmem = pl.BlockSpec(memory_space=pltpu.VMEM)
    half = jax.ShapeDtypeStruct((2 * rows, 16 * rows), jnp.float32)
    padded = (4 * rows + 127) // 128 * 128
    return pl.pallas_call(
        functools.partial(gram_kernel, rows),
        out_shape=(half, half),
        in_specs=[vmem] * 6,
        out_specs=(vmem, vmem),
        scratch_shapes=[
            pltpu.VMEM((4 * rows, pieces[-1].shape[1]), jnp.bfloat16),
            pltpu.VMEM((16 * rows, padded), jnp.float32),
        ],
        compiler_params=pltpu.CompilerParams(vmem_limit_bytes=16 * 1024 * 1024),
    )(*pieces)


def mixer_kernel(rows, mine, other, *refs):
    outputs, (straight, flip, moved) = refs[:2], refs[2:]
    _, z, _ = position()
    for k in range(2):
        for half, ref in enumerate((mine, other)):
            at = pl.multiple_of(((2 * (kept_half() ^ half) + k) ^ z) * rows, rows)
            straight[pl.ds(at, rows), :] = ref[k * rows : (k + 1) * rows, :].astype(jnp.float32)
    straight[4 * rows :, :] = jnp.zeros((straight.shape[0] - 4 * rows, 16 * rows), jnp.float32)
    flip[...] = straight[...].T
    for part, ref in enumerate(outputs):
        for k, place in enumerate(gathered_places(part)):
            at = pl.multiple_of(place * rows, rows)
            moved[k * rows : (k + 1) * rows, :] = flip[pl.ds(at, rows), :]
        ref[...] = moved[...].T[0 : 4 * rows].astype(jnp.bfloat16)


def mixer_parts(rows, mine, other):
    vmem = pl.BlockSpec(memory_space=pltpu.VMEM)
    shape = jax.ShapeDtypeStruct((4 * rows, 16 * rows), jnp.bfloat16)
    padded = (4 * rows + 127) // 128 * 128
    return pl.pallas_call(
        functools.partial(mixer_kernel, rows),
        out_shape=(shape, shape),
        in_specs=[vmem] * 2,
        out_specs=(vmem, vmem),
        scratch_shapes=[
            pltpu.VMEM((padded, 16 * rows), jnp.float32),
            pltpu.VMEM((16 * rows, padded), jnp.float32),
            pltpu.VMEM((16 * rows, padded), jnp.float32),
        ],
        compiler_params=pltpu.CompilerParams(vmem_limit_bytes=8 * 1024 * 1024),
    )(mine, other)


def per_device(gradient):
    rows, cols = gradient.shape
    y, x, z = (lax.axis_index(k) for k in ("y", "x", "z"))
    zl, core = lax.axis_index("zl"), lax.axis_index("core")
    plane = y * 4 + x

    half = core ^ (z >> 1)
    choices = (half == 0, zl == (z & 1), core == 0, (z - 2 * half) * rows, plane * rows)
    gradient, choices = lax.optimization_barrier((gradient, choices))
    first_half, first_block, first_core, first_row, first_column = choices

    middle = cols // 2 // 128 * 128
    one_z = swap_z(gradient, (1, 3))
    one_z, other_z = lax.optimization_barrier((one_z, swap_z(gradient, (3, 1))))
    far_z = [other_z, swap_z(one_z, (3, 1))]
    parts = [gradient[:, :middle], gradient[:, middle:]]
    for step in range(3):
        parts = [
            jnp.concatenate([value, swap_plane(value, part, step)], 0)
            for part, value in enumerate(parts)
        ]
    pieces = []
    for part, value in enumerate(parts):
        pieces += [value, swap_plane(value, part, 3)]
    pieces += [jnp.concatenate([gradient, one_z], 0), jnp.concatenate(far_z, 0)]
    pieces = lax.optimization_barrier(pieces)

    width = 16 * rows

    row = lax.broadcasted_iota(jnp.int32, (2 * rows, width), 0) - first_row
    column = lax.broadcasted_iota(jnp.int32, (2 * rows, width), 1) - first_column
    diagonal = (row == column) & (row >= 0) & (row < rows)

    def add_zl(value):
        rounded = lax.reduce_precision(value, 8, 7)
        rest = jnp.sum(jnp.where(diagonal, value - rounded, 0.0), 0, keepdims=True)
        rest = jnp.broadcast_to(rest, (16, width))
        sent = jnp.concatenate([rounded, rest]).astype(jnp.bfloat16)
        got = swap_zl(sent).astype(jnp.float32)
        return value + got[: 2 * rows] + jnp.where(diagonal, got[2 * rows : 2 * rows + 1], 0.0)

    gram_half, given = gram_halves(rows, pieces)
    gram_half = add_zl(gram_half + swap_core(given)).astype(jnp.bfloat16)

    right = jnp.where(first_block, gram_half[:rows], gram_half[rows:])
    right = lax.all_to_all(
        jnp.broadcast_to(right[None], (16, rows, width)), ("y", "x"), 0, 0
    ).reshape(width, width)
    other = swap_core(gram_half)
    left = exchange(
        jnp.where(
            first_half, jnp.concatenate([gram_half, other]), jnp.concatenate([other, gram_half])
        ),
        lambda y, x, z, zl, core: (y, x, z ^ (2 * core + zl), zl, core),
    )
    square = jnp.dot(left, right, preferred_element_type=jnp.float32)
    halves = square[: 2 * rows], square[2 * rows :]
    square = jnp.where(first_half, halves[0], halves[1])
    square = add_zl(square + swap_core(jnp.where(first_half, halves[1], halves[0])))
    mixer = (coef_b * gram_half.astype(jnp.float32) + coef_c * square).astype(jnp.bfloat16)
    mixers = mixer_parts(rows, mixer, swap_core(mixer))

    sums = []
    for part, block in enumerate(mixers):
        product = jnp.dot(
            block[:, : 8 * rows], pieces[2 * part], preferred_element_type=jnp.float32
        ) + jnp.dot(
            block[:, 8 * rows :], pieces[2 * part + 1], preferred_element_type=jnp.float32
        )
        product = product.reshape(4, rows, product.shape[1])
        near = jnp.where(first_core, product[1], product[3])
        far = jnp.where(first_core, product[3], product[1])
        moved = swap_z(jnp.stack([far, product[2]]).astype(jnp.bfloat16), (3, 1))
        moved = moved.astype(jnp.float32)
        last = swap_z((near + moved[1]).astype(jnp.bfloat16), (1, 3))
        sums.append(product[0] + moved[0] + last.astype(jnp.float32))
    combined = coef_a * gradient.astype(jnp.float32) + jnp.concatenate(sums, 1)
    factor = math.sqrt(float(cols * 4))
    return (combined * factor).astype(jnp.bfloat16)


def solution(mesh):
    split = Mesh(mesh.devices.reshape(SIZES), ALL)
    spec = P(("y", "x", "z"), ("zl", "core"))
    return jax.shard_map(
        per_device, mesh=split, in_specs=(spec,), out_specs=spec, check_vma=False
    )
```

```python
import functools
import math

import jax
import jax.numpy as jnp
import numpy as np
from jax import lax
from jax.experimental import pallas as pl
from jax.experimental.pallas import tpu as pltpu
from jax.sharding import Mesh, PartitionSpec as P

coef_a = 3.4445
coef_b = -4.775
coef_c = 2.0315

ALL = ("y", "x", "z", "zl", "core")
SIZES = (4, 4, 4, 2, 2)

STEP_MASKS = (4, 1, 12, 3)
Z_MASKS = ((1, 3), (3, 1))


def partners(function):
    pairs = []
    for i in range(math.prod(SIZES)):
        there = function(*(int(k) for k in np.unravel_index(i, SIZES)))
        pairs.append((i, int(np.ravel_multi_index(there, SIZES))))
    return pairs


def exchange(value, function):
    return lax.ppermute(value, ALL, partners(function))


def plane_mask(core, part, step):
    return STEP_MASKS[(step + 2 * core + part) % 4]


def swap_plane(value, part, step):
    def there(y, x, z, zl, core):
        mask = plane_mask(core, part, step)
        return y ^ (mask >> 2), x ^ (mask & 3), z, zl, core

    return exchange(value, there)


def swap_z(value, masks):
    return exchange(value, lambda y, x, z, zl, core: (y, x, z ^ masks[core], zl, core))


def swap_core(value):
    return exchange(value, lambda y, x, z, zl, core: (y, x, z, zl, core ^ 1))


def swap_zl(value):
    return exchange(value, lambda y, x, z, zl, core: (y, x, z, zl ^ 1, core))


def offsets(masks):
    found = [0]
    for mask in masks:
        found = found + [k ^ mask for k in found]
    return found


def multiply(a, b, dims):
    return lax.dot_general(a, b, (dims, ((), ())), preferred_element_type=jnp.float32)


def position():
    y, x, z, core = (lax.axis_index(k) for k in ("y", "x", "z", "core"))
    return y * 4 + x, z, core


def gathered_places(part):
    plane, _, core = position()
    orders = [offsets([plane_mask(c, part, step) for step in range(4)]) for c in range(2)]
    return [plane ^ jnp.where(core == 0, *pair) for pair in zip(*orders)]


def kept_half():
    _, z, core = position()
    return core ^ (z >> 1)


def gram_kernel(rows, c00, c01, c10, c11, near, far, *refs):
    keep, give, own, flip = refs
    _, z, core = position()
    orders = [offsets(masks) for masks in Z_MASKS]
    for k, pair in enumerate(zip(*orders)):
        at = pl.multiple_of((z ^ jnp.where(core == 0, *pair)) * rows, rows)
        ref = (near, far)[k // 2]
        own[pl.ds(at, rows), :] = ref[(k % 2) * rows : (k % 2 + 1) * rows, :]
    flip[:, 4 * rows :] = jnp.zeros((16 * rows, flip.shape[1] - 4 * rows), jnp.float32)
    start = 0
    for part, halves in enumerate(((c00, c01), (c10, c11))):
        width = halves[0].shape[1]
        places = gathered_places(part)
        for half in range(2):
            block = multiply(halves[half][...], own[:, start : start + width], ((1,), (1,)))
            for k in range(8):
                at = pl.multiple_of(places[8 * half + k] * rows, rows)
                value = block[k * rows : (k + 1) * rows, :]
                if part > 0:
                    value = value + flip[pl.ds(at, rows), 0 : 4 * rows]
                flip[pl.ds(at, rows), 0 : 4 * rows] = value
        start += width
    gram = flip[...].T
    first = kept_half() == 0
    keep[...] = jnp.where(first, gram[0 : 2 * rows], gram[2 * rows : 4 * rows])
    give[...] = jnp.where(first, gram[2 * rows : 4 * rows], gram[0 : 2 * rows])


def gram_halves(rows, pieces):
    vmem = pl.BlockSpec(memory_space=pltpu.VMEM)
    half = jax.ShapeDtypeStruct((2 * rows, 16 * rows), jnp.float32)
    padded = (4 * rows + 127) // 128 * 128
    return pl.pallas_call(
        functools.partial(gram_kernel, rows),
        out_shape=(half, half),
        in_specs=[vmem] * 6,
        out_specs=(vmem, vmem),
        scratch_shapes=[
            pltpu.VMEM((4 * rows, pieces[-1].shape[1]), jnp.bfloat16),
            pltpu.VMEM((16 * rows, padded), jnp.float32),
        ],
        compiler_params=pltpu.CompilerParams(vmem_limit_bytes=16 * 1024 * 1024),
    )(*pieces)


def mixer_kernel(rows, mine, other, *refs):
    outputs, (straight, flip, moved) = refs[:2], refs[2:]
    _, z, _ = position()
    for k in range(2):
        for half, ref in enumerate((mine, other)):
            at = pl.multiple_of(((2 * (kept_half() ^ half) + k) ^ z) * rows, rows)
            straight[pl.ds(at, rows), :] = ref[k * rows : (k + 1) * rows, :].astype(jnp.float32)
    straight[4 * rows :, :] = jnp.zeros((straight.shape[0] - 4 * rows, 16 * rows), jnp.float32)
    flip[...] = straight[...].T
    for part, ref in enumerate(outputs):
        for k, place in enumerate(gathered_places(part)):
            at = pl.multiple_of(place * rows, rows)
            moved[k * rows : (k + 1) * rows, :] = flip[pl.ds(at, rows), :]
        ref[...] = moved[...].T[0 : 4 * rows].astype(jnp.bfloat16)


def mixer_parts(rows, mine, other):
    vmem = pl.BlockSpec(memory_space=pltpu.VMEM)
    shape = jax.ShapeDtypeStruct((4 * rows, 16 * rows), jnp.bfloat16)
    padded = (4 * rows + 127) // 128 * 128
    return pl.pallas_call(
        functools.partial(mixer_kernel, rows),
        out_shape=(shape, shape),
        in_specs=[vmem] * 2,
        out_specs=(vmem, vmem),
        scratch_shapes=[
            pltpu.VMEM((padded, 16 * rows), jnp.float32),
            pltpu.VMEM((16 * rows, padded), jnp.float32),
            pltpu.VMEM((16 * rows, padded), jnp.float32),
        ],
        compiler_params=pltpu.CompilerParams(vmem_limit_bytes=8 * 1024 * 1024),
    )(mine, other)


def per_device(gradient):
    rows, cols = gradient.shape
    y, x, z = (lax.axis_index(k) for k in ("y", "x", "z"))
    zl, core = lax.axis_index("zl"), lax.axis_index("core")
    plane = y * 4 + x

    half = core ^ (z >> 1)
    choices = (half == 0, zl == (z & 1), core == 0, (z - 2 * half) * rows, plane * rows)
    gradient, choices = lax.optimization_barrier((gradient, choices))
    first_half, first_block, first_core, first_row, first_column = choices

    middle = cols // 2 // 128 * 128
    one_z = swap_z(gradient, (1, 3))
    one_z, other_z = lax.optimization_barrier((one_z, swap_z(gradient, (3, 1))))
    far_z = [other_z, swap_z(one_z, (3, 1))]
    parts = [gradient[:, :middle], gradient[:, middle:]]
    for step in range(3):
        parts = [
            jnp.concatenate([value, swap_plane(value, part, step)], 0)
            for part, value in enumerate(parts)
        ]
    pieces = []
    for part, value in enumerate(parts):
        pieces += [value, swap_plane(value, part, 3)]
    pieces += [jnp.concatenate([gradient, one_z], 0), jnp.concatenate(far_z, 0)]
    pieces = lax.optimization_barrier(pieces)

    width = 16 * rows

    row = lax.broadcasted_iota(jnp.int32, (2 * rows, width), 0) - first_row
    column = lax.broadcasted_iota(jnp.int32, (2 * rows, width), 1) - first_column
    diagonal = (row == column) & (row >= 0) & (row < rows)

    def add_zl(value):
        rounded = lax.reduce_precision(value, 8, 7)
        rest = jnp.sum(jnp.where(diagonal, value - rounded, 0.0), 0, keepdims=True)
        rest = jnp.broadcast_to(rest, (16, width))
        sent = jnp.concatenate([rounded, rest]).astype(jnp.bfloat16)
        got = swap_zl(sent).astype(jnp.float32)
        return value + got[: 2 * rows] + jnp.where(diagonal, got[2 * rows : 2 * rows + 1], 0.0)

    gram_half, given = gram_halves(rows, pieces)
    gram_half = add_zl(gram_half + swap_core(given)).astype(jnp.bfloat16)

    right = jnp.where(first_block, gram_half[:rows], gram_half[rows:])
    right = lax.all_to_all(
        jnp.broadcast_to(right[None], (16, rows, width)), ("y", "x"), 0, 0
    ).reshape(width, width)
    other = swap_core(gram_half)
    left = exchange(
        jnp.where(
            first_half, jnp.concatenate([gram_half, other]), jnp.concatenate([other, gram_half])
        ),
        lambda y, x, z, zl, core: (y, x, z ^ (2 * core + zl), zl, core),
    )
    square = jnp.dot(left, right, preferred_element_type=jnp.float32)
    halves = square[: 2 * rows], square[2 * rows :]
    square = jnp.where(first_half, halves[0], halves[1])
    square = add_zl(square + swap_core(jnp.where(first_half, halves[1], halves[0])))
    mixer = (coef_b * gram_half.astype(jnp.float32) + coef_c * square).astype(jnp.bfloat16)
    mixers = mixer_parts(rows, mixer, swap_core(mixer))

    sums = []
    for part, block in enumerate(mixers):
        product = jnp.dot(
            block[:, : 8 * rows], pieces[2 * part], preferred_element_type=jnp.float32
        ) + jnp.dot(
            block[:, 8 * rows :], pieces[2 * part + 1], preferred_element_type=jnp.float32
        )
        product = product.reshape(4, rows, product.shape[1])
        near = jnp.where(first_core, product[1], product[3])
        far = jnp.where(first_core, product[3], product[1])
        moved = swap_z(product[2].astype(jnp.bfloat16), (3, 1)).astype(jnp.float32)
        total = product[0] + swap_z(far.astype(jnp.bfloat16), (3, 1)).astype(jnp.float32)
        last = swap_z((near + moved).astype(jnp.bfloat16), (1, 3))
        sums.append(total + last.astype(jnp.float32))
    combined = coef_a * gradient.astype(jnp.float32) + jnp.concatenate(sums, 1)
    factor = math.sqrt(float(cols * 4))
    return (combined * factor).astype(jnp.bfloat16)


def solution(mesh):
    split = Mesh(mesh.devices.reshape(SIZES), ALL)
    spec = P(("y", "x", "z"), ("zl", "core"))
    return jax.shard_map(
        per_device, mesh=split, in_specs=(spec,), out_specs=spec, check_vma=False
    )
```

```python
import functools
import math

import jax
import jax.numpy as jnp
import numpy as np
from jax import lax
from jax.experimental import pallas as pl
from jax.experimental.pallas import tpu as pltpu
from jax.sharding import Mesh, PartitionSpec as P

coef_a = 3.4445
coef_b = -4.775
coef_c = 2.0315

ALL = ("y", "x", "z", "zl", "core")
SIZES = (4, 4, 4, 2, 2)

STEP_MASKS = (4, 1, 12, 3)
Z_MASKS = ((1, 3), (3, 1))


def partners(function):
    pairs = []
    for i in range(math.prod(SIZES)):
        there = function(*(int(k) for k in np.unravel_index(i, SIZES)))
        pairs.append((i, int(np.ravel_multi_index(there, SIZES))))
    return pairs


def exchange(value, function):
    return lax.ppermute(value, ALL, partners(function))


def plane_mask(core, part, step):
    return STEP_MASKS[(step + 2 * core + part) % 4]


def swap_plane(value, part, step):
    def there(y, x, z, zl, core):
        mask = plane_mask(core, part, step)
        return y ^ (mask >> 2), x ^ (mask & 3), z, zl, core

    return exchange(value, there)


def swap_z(value, masks):
    return exchange(value, lambda y, x, z, zl, core: (y, x, z ^ masks[core], zl, core))


def swap_core(value):
    return exchange(value, lambda y, x, z, zl, core: (y, x, z, zl, core ^ 1))


def swap_zl(value):
    return exchange(value, lambda y, x, z, zl, core: (y, x, z, zl ^ 1, core))


def offsets(masks):
    found = [0]
    for mask in masks:
        found = found + [k ^ mask for k in found]
    return found


def multiply(a, b, dims):
    return lax.dot_general(a, b, (dims, ((), ())), preferred_element_type=jnp.float32)


def position():
    y, x, z, core = (lax.axis_index(k) for k in ("y", "x", "z", "core"))
    return y * 4 + x, z, core


def gathered_places(part):
    plane, _, core = position()
    orders = [offsets([plane_mask(c, part, step) for step in range(4)]) for c in range(2)]
    return [plane ^ jnp.where(core == 0, *pair) for pair in zip(*orders)]


def kept_half():
    _, z, core = position()
    return core ^ (z >> 1)


def gram_kernel(rows, c00, c01, c10, c11, near, far, *refs):
    keep, give, own, flip = refs
    _, z, core = position()
    orders = [offsets(masks) for masks in Z_MASKS]
    for k, pair in enumerate(zip(*orders)):
        at = pl.multiple_of((z ^ jnp.where(core == 0, *pair)) * rows, rows)
        ref = (near, far)[k // 2]
        own[pl.ds(at, rows), :] = ref[(k % 2) * rows : (k % 2 + 1) * rows, :]
    flip[:, 4 * rows :] = jnp.zeros((16 * rows, flip.shape[1] - 4 * rows), jnp.float32)
    start = 0
    for part, halves in enumerate(((c00, c01), (c10, c11))):
        width = halves[0].shape[1]
        places = gathered_places(part)
        for half in range(2):
            block = multiply(halves[half][...], own[:, start : start + width], ((1,), (1,)))
            for k in range(8):
                at = pl.multiple_of(places[8 * half + k] * rows, rows)
                value = block[k * rows : (k + 1) * rows, :]
                if part > 0:
                    value = value + flip[pl.ds(at, rows), 0 : 4 * rows]
                flip[pl.ds(at, rows), 0 : 4 * rows] = value
        start += width
    gram = flip[...].T
    first = kept_half() == 0
    keep[...] = jnp.where(first, gram[0 : 2 * rows], gram[2 * rows : 4 * rows])
    give[...] = jnp.where(first, gram[2 * rows : 4 * rows], gram[0 : 2 * rows])


def gram_halves(rows, pieces):
    vmem = pl.BlockSpec(memory_space=pltpu.VMEM)
    half = jax.ShapeDtypeStruct((2 * rows, 16 * rows), jnp.float32)
    padded = (4 * rows + 127) // 128 * 128
    return pl.pallas_call(
        functools.partial(gram_kernel, rows),
        out_shape=(half, half),
        in_specs=[vmem] * 6,
        out_specs=(vmem, vmem),
        scratch_shapes=[
            pltpu.VMEM((4 * rows, pieces[-1].shape[1]), jnp.bfloat16),
            pltpu.VMEM((16 * rows, padded), jnp.float32),
        ],
        compiler_params=pltpu.CompilerParams(vmem_limit_bytes=16 * 1024 * 1024),
    )(*pieces)


def mixer_kernel(rows, mine, other, *refs):
    outputs, (straight, flip, moved) = refs[:2], refs[2:]
    _, z, _ = position()
    for k in range(2):
        for half, ref in enumerate((mine, other)):
            at = pl.multiple_of(((2 * (kept_half() ^ half) + k) ^ z) * rows, rows)
            straight[pl.ds(at, rows), :] = ref[k * rows : (k + 1) * rows, :].astype(jnp.float32)
    straight[4 * rows :, :] = jnp.zeros((straight.shape[0] - 4 * rows, 16 * rows), jnp.float32)
    flip[...] = straight[...].T
    for part, ref in enumerate(outputs):
        for k, place in enumerate(gathered_places(part)):
            at = pl.multiple_of(place * rows, rows)
            moved[k * rows : (k + 1) * rows, :] = flip[pl.ds(at, rows), :]
        ref[...] = moved[...].T[0 : 4 * rows].astype(jnp.bfloat16)


def mixer_parts(rows, mine, other):
    vmem = pl.BlockSpec(memory_space=pltpu.VMEM)
    shape = jax.ShapeDtypeStruct((4 * rows, 16 * rows), jnp.bfloat16)
    padded = (4 * rows + 127) // 128 * 128
    return pl.pallas_call(
        functools.partial(mixer_kernel, rows),
        out_shape=(shape, shape),
        in_specs=[vmem] * 2,
        out_specs=(vmem, vmem),
        scratch_shapes=[
            pltpu.VMEM((padded, 16 * rows), jnp.float32),
            pltpu.VMEM((16 * rows, padded), jnp.float32),
            pltpu.VMEM((16 * rows, padded), jnp.float32),
        ],
        compiler_params=pltpu.CompilerParams(vmem_limit_bytes=8 * 1024 * 1024),
    )(mine, other)


def per_device(gradient):
    rows, cols = gradient.shape
    y, x, z = (lax.axis_index(k) for k in ("y", "x", "z"))
    zl, core = lax.axis_index("zl"), lax.axis_index("core")
    plane = y * 4 + x

    half = core ^ (z >> 1)
    choices = (half == 0, zl == (z & 1), core == 0, (z - 2 * half) * rows, plane * rows)
    gradient, choices = lax.optimization_barrier((gradient, choices))
    first_half, first_block, first_core, first_row, first_column = choices

    middle = cols // 2 // 128 * 128
    one_z = swap_z(gradient, (1, 3))
    one_z, other_z = lax.optimization_barrier((one_z, swap_z(gradient, (3, 1))))
    last_z = swap_z(one_z[:, :middle], (3, 1)), swap_z(other_z[:, middle:], (1, 3))
    far_z = [other_z, jnp.concatenate(last_z, 1)]
    parts = [gradient[:, :middle], gradient[:, middle:]]
    for step in range(3):
        parts = [
            jnp.concatenate([value, swap_plane(value, part, step)], 0)
            for part, value in enumerate(parts)
        ]
    pieces = []
    for part, value in enumerate(parts):
        pieces += [value, swap_plane(value, part, 3)]
    pieces += [jnp.concatenate([gradient, one_z], 0), jnp.concatenate(far_z, 0)]
    pieces = lax.optimization_barrier(pieces)

    width = 16 * rows

    row = lax.broadcasted_iota(jnp.int32, (2 * rows, width), 0) - first_row
    column = lax.broadcasted_iota(jnp.int32, (2 * rows, width), 1) - first_column
    diagonal = (row == column) & (row >= 0) & (row < rows)

    def add_zl(value):
        rounded = lax.reduce_precision(value, 8, 7)
        rest = jnp.sum(jnp.where(diagonal, value - rounded, 0.0), 0, keepdims=True)
        rest = jnp.broadcast_to(rest, (16, width))
        sent = jnp.concatenate([rounded, rest]).astype(jnp.bfloat16)
        got = swap_zl(sent).astype(jnp.float32)
        return value + got[: 2 * rows] + jnp.where(diagonal, got[2 * rows : 2 * rows + 1], 0.0)

    gram_half, given = gram_halves(rows, pieces)
    gram_half = add_zl(gram_half + swap_core(given)).astype(jnp.bfloat16)

    right = jnp.where(first_block, gram_half[:rows], gram_half[rows:])
    right = lax.all_to_all(
        jnp.broadcast_to(right[None], (16, rows, width)), ("y", "x"), 0, 0
    ).reshape(width, width)
    other = swap_core(gram_half)
    left = exchange(
        jnp.where(
            first_half, jnp.concatenate([gram_half, other]), jnp.concatenate([other, gram_half])
        ),
        lambda y, x, z, zl, core: (y, x, z ^ (2 * core + zl), zl, core),
    )
    square = jnp.dot(left, right, preferred_element_type=jnp.float32)
    halves = square[: 2 * rows], square[2 * rows :]
    square = jnp.where(first_half, halves[0], halves[1])
    square = add_zl(square + swap_core(jnp.where(first_half, halves[1], halves[0])))
    mixer = (coef_b * gram_half.astype(jnp.float32) + coef_c * square).astype(jnp.bfloat16)
    mixers = mixer_parts(rows, mixer, swap_core(mixer))

    sums = []
    for part, block in enumerate(mixers):
        product = jnp.dot(
            block[:, : 8 * rows], pieces[2 * part], preferred_element_type=jnp.float32
        ) + jnp.dot(
            block[:, 8 * rows :], pieces[2 * part + 1], preferred_element_type=jnp.float32
        )
        product = product.reshape(4, rows, product.shape[1])
        one, three = (1, 3) if part == 0 else (3, 1)
        near = jnp.where(first_core, product[one], product[three])
        far = jnp.where(first_core, product[three], product[one])
        moved = swap_z(product[2].astype(jnp.bfloat16), (three, one)).astype(jnp.float32)
        far = swap_z(far.astype(jnp.bfloat16), (three, one)).astype(jnp.float32)
        last = swap_z((near + moved).astype(jnp.bfloat16), (one, three))
        total = product[0] + far
        sums.append(total + last.astype(jnp.float32))
    combined = coef_a * gradient.astype(jnp.float32) + jnp.concatenate(sums, 1)
    factor = math.sqrt(float(cols * 4))
    return (combined * factor).astype(jnp.bfloat16)


def solution(mesh):
    split = Mesh(mesh.devices.reshape(SIZES), ALL)
    spec = P(("y", "x", "z"), ("zl", "core"))
    return jax.shard_map(
        per_device, mesh=split, in_specs=(spec,), out_specs=spec, check_vma=False
    )
```

```python
import functools
import math

import jax
import jax.numpy as jnp
import numpy as np
from jax import lax
from jax.experimental import pallas as pl
from jax.experimental.pallas import tpu as pltpu
from jax.sharding import Mesh, PartitionSpec as P

coef_a = 3.4445
coef_b = -4.775
coef_c = 2.0315

ALL = ("y", "x", "z", "zl", "core")
SIZES = (4, 4, 4, 2, 2)

STEP_MASKS = (4, 1, 12, 3)
Z_MASKS = ((1, 3), (3, 1))


def partners(function):
    pairs = []
    for i in range(math.prod(SIZES)):
        there = function(*(int(k) for k in np.unravel_index(i, SIZES)))
        pairs.append((i, int(np.ravel_multi_index(there, SIZES))))
    return pairs


def exchange(value, function):
    return lax.ppermute(value, ALL, partners(function))


def plane_mask(core, part, step):
    return STEP_MASKS[(step + 2 * core + part) % 4]


def swap_plane(value, part, step):
    def there(y, x, z, zl, core):
        mask = plane_mask(core, part, step)
        return y ^ (mask >> 2), x ^ (mask & 3), z, zl, core

    return exchange(value, there)


def swap_z(value, masks):
    return exchange(value, lambda y, x, z, zl, core: (y, x, z ^ masks[core], zl, core))


def swap_core(value):
    return exchange(value, lambda y, x, z, zl, core: (y, x, z, zl, core ^ 1))


def swap_zl(value):
    return exchange(value, lambda y, x, z, zl, core: (y, x, z, zl ^ 1, core))


def offsets(masks):
    found = [0]
    for mask in masks:
        found = found + [k ^ mask for k in found]
    return found


def multiply(a, b, dims):
    return lax.dot_general(a, b, (dims, ((), ())), preferred_element_type=jnp.float32)


def position():
    y, x, z, core = (lax.axis_index(k) for k in ("y", "x", "z", "core"))
    return y * 4 + x, z, core


def gathered_places(part):
    plane, _, core = position()
    orders = [offsets([plane_mask(c, part, step) for step in range(4)]) for c in range(2)]
    return [plane ^ jnp.where(core == 0, *pair) for pair in zip(*orders)]


def kept_half():
    _, z, core = position()
    return core ^ (z >> 1)


def gram_kernel(rows, c00, c01, c10, c11, near, far, *refs):
    keep, give, own, flip = refs
    _, z, core = position()
    orders = [offsets(masks) for masks in Z_MASKS]
    for k, pair in enumerate(zip(*orders)):
        at = pl.multiple_of((z ^ jnp.where(core == 0, *pair)) * rows, rows)
        ref = (near, far)[k // 2]
        own[pl.ds(at, rows), :] = ref[(k % 2) * rows : (k % 2 + 1) * rows, :]
    flip[:, 4 * rows :] = jnp.zeros((16 * rows, flip.shape[1] - 4 * rows), jnp.float32)
    start = 0
    for part, halves in enumerate(((c00, c01), (c10, c11))):
        width = halves[0].shape[1]
        places = gathered_places(part)
        for half in range(2):
            block = multiply(halves[half][...], own[:, start : start + width], ((1,), (1,)))
            for k in range(8):
                at = pl.multiple_of(places[8 * half + k] * rows, rows)
                value = block[k * rows : (k + 1) * rows, :]
                if part > 0:
                    value = value + flip[pl.ds(at, rows), 0 : 4 * rows]
                flip[pl.ds(at, rows), 0 : 4 * rows] = value
        start += width
    gram = flip[...].T
    first = kept_half() == 0
    keep[...] = jnp.where(first, gram[0 : 2 * rows], gram[2 * rows : 4 * rows])
    give[...] = jnp.where(first, gram[2 * rows : 4 * rows], gram[0 : 2 * rows])


def gram_halves(rows, pieces):
    vmem = pl.BlockSpec(memory_space=pltpu.VMEM)
    half = jax.ShapeDtypeStruct((2 * rows, 16 * rows), jnp.float32)
    padded = (4 * rows + 127) // 128 * 128
    return pl.pallas_call(
        functools.partial(gram_kernel, rows),
        out_shape=(half, half),
        in_specs=[vmem] * 6,
        out_specs=(vmem, vmem),
        scratch_shapes=[
            pltpu.VMEM((4 * rows, pieces[-1].shape[1]), jnp.bfloat16),
            pltpu.VMEM((16 * rows, padded), jnp.float32),
        ],
        compiler_params=pltpu.CompilerParams(vmem_limit_bytes=16 * 1024 * 1024),
    )(*pieces)


def mixer_kernel(rows, mine, other, *refs):
    outputs, (straight, flip, moved) = refs[:2], refs[2:]
    _, z, _ = position()
    for k in range(2):
        for half, ref in enumerate((mine, other)):
            at = pl.multiple_of(((2 * (kept_half() ^ half) + k) ^ z) * rows, rows)
            straight[pl.ds(at, rows), :] = ref[k * rows : (k + 1) * rows, :].astype(jnp.float32)
    straight[4 * rows :, :] = jnp.zeros((straight.shape[0] - 4 * rows, 16 * rows), jnp.float32)
    flip[...] = straight[...].T
    for part, ref in enumerate(outputs):
        for k, place in enumerate(gathered_places(part)):
            at = pl.multiple_of(place * rows, rows)
            moved[k * rows : (k + 1) * rows, :] = flip[pl.ds(at, rows), :]
        ref[...] = moved[...].T[0 : 4 * rows].astype(jnp.bfloat16)


def mixer_parts(rows, mine, other):
    vmem = pl.BlockSpec(memory_space=pltpu.VMEM)
    shape = jax.ShapeDtypeStruct((4 * rows, 16 * rows), jnp.bfloat16)
    padded = (4 * rows + 127) // 128 * 128
    return pl.pallas_call(
        functools.partial(mixer_kernel, rows),
        out_shape=(shape, shape),
        in_specs=[vmem] * 2,
        out_specs=(vmem, vmem),
        scratch_shapes=[
            pltpu.VMEM((padded, 16 * rows), jnp.float32),
            pltpu.VMEM((16 * rows, padded), jnp.float32),
            pltpu.VMEM((16 * rows, padded), jnp.float32),
        ],
        compiler_params=pltpu.CompilerParams(vmem_limit_bytes=8 * 1024 * 1024),
    )(mine, other)


def per_device(gradient):
    rows, cols = gradient.shape
    y, x, z = (lax.axis_index(k) for k in ("y", "x", "z"))
    zl, core = lax.axis_index("zl"), lax.axis_index("core")
    plane = y * 4 + x

    half = core ^ (z >> 1)
    choices = (half == 0, zl == (z & 1), core == 0, (z - 2 * half) * rows, plane * rows)
    gradient, choices = lax.optimization_barrier((gradient, choices))
    first_half, first_block, first_core, first_row, first_column = choices

    middle = cols // 2 // 128 * 128
    one_z = swap_z(gradient, (1, 3))
    one_z, other_z = lax.optimization_barrier((one_z, swap_z(gradient, (3, 1))))
    last_z = swap_z(one_z[:, :middle], (3, 1)), swap_z(other_z[:, middle:], (1, 3))
    far_z = [other_z, jnp.concatenate(last_z, 1)]
    parts = [gradient[:, :middle], gradient[:, middle:]]
    for step in range(3):
        parts = [
            jnp.concatenate([value, swap_plane(value, part, step)], 0)
            for part, value in enumerate(parts)
        ]
    pieces = []
    for part, value in enumerate(parts):
        pieces += [value, swap_plane(value, part, 3)]
    pieces += [jnp.concatenate([gradient, one_z], 0), jnp.concatenate(far_z, 0)]
    pieces = lax.optimization_barrier(pieces)

    width = 16 * rows

    row = lax.broadcasted_iota(jnp.int32, (2 * rows, width), 0) - first_row
    column = lax.broadcasted_iota(jnp.int32, (2 * rows, width), 1) - first_column
    diagonal = (row == column) & (row >= 0) & (row < rows)

    def add_zl(value):
        rounded = lax.reduce_precision(value, 8, 7)
        rest = jnp.sum(jnp.where(diagonal, value - rounded, 0.0), 0, keepdims=True)
        rest = jnp.broadcast_to(rest, (16, width))
        sent = jnp.concatenate([rounded, rest]).astype(jnp.bfloat16)
        got = swap_zl(sent).astype(jnp.float32)
        return value + got[: 2 * rows] + jnp.where(diagonal, got[2 * rows : 2 * rows + 1], 0.0)

    gram_half, given = gram_halves(rows, pieces)
    gram_half = add_zl(gram_half + swap_core(given)).astype(jnp.bfloat16)

    right = jnp.where(first_block, gram_half[:rows], gram_half[rows:])
    right = lax.all_to_all(
        jnp.broadcast_to(right[None], (16, rows, width)), ("y", "x"), 0, 0
    ).reshape(width, width)
    other = swap_core(gram_half)
    left = exchange(
        jnp.where(
            first_half, jnp.concatenate([gram_half, other]), jnp.concatenate([other, gram_half])
        ),
        lambda y, x, z, zl, core: (y, x, z ^ (2 * core + zl), zl, core),
    )
    square = jnp.dot(left, right, preferred_element_type=jnp.float32)
    halves = square[: 2 * rows], square[2 * rows :]
    square = jnp.where(first_half, halves[0], halves[1])
    square = add_zl(square + swap_core(jnp.where(first_half, halves[1], halves[0])))
    mixer = (coef_b * gram_half.astype(jnp.float32) + coef_c * square).astype(jnp.bfloat16)
    mixers = mixer_parts(rows, mixer, swap_core(mixer))

    sums = []
    for part, block in reversed(list(enumerate(mixers))):
        product = jnp.dot(
            block[:, : 8 * rows], pieces[2 * part], preferred_element_type=jnp.float32
        ) + jnp.dot(
            block[:, 8 * rows :], pieces[2 * part + 1], preferred_element_type=jnp.float32
        )
        product = product.reshape(4, rows, product.shape[1])
        one, three = (1, 3) if part == 0 else (3, 1)
        near = jnp.where(first_core, product[one], product[three])
        far = jnp.where(first_core, product[three], product[one])
        moved = swap_z(product[2].astype(jnp.bfloat16), (three, one)).astype(jnp.float32)
        far = swap_z(far.astype(jnp.bfloat16), (three, one)).astype(jnp.float32)
        last = swap_z((near + moved).astype(jnp.bfloat16), (one, three))
        total = product[0] + far
        sums.append(total + last.astype(jnp.float32))
    combined = coef_a * gradient.astype(jnp.float32) + jnp.concatenate(sums[::-1], 1)
    factor = math.sqrt(float(cols * 4))
    return (combined * factor).astype(jnp.bfloat16)


def solution(mesh):
    split = Mesh(mesh.devices.reshape(SIZES), ALL)
    spec = P(("y", "x", "z"), ("zl", "core"))
    return jax.shard_map(
        per_device, mesh=split, in_specs=(spec,), out_specs=spec, check_vma=False
    )
```
